256 devices in a mesh: area: 16 (over x_lo, z), tile: 16 (over y, x_hi, core).
Axes of the slice: x: 4 (x_hi: 2, x_lo: 2; x = x_hi * 2 + x_lo), y: 4, z: 8, core: 2. Of those that a mesh axis runs over, the one named last changes fastest.
Arguments:
- start_rates: bfloat16 [16, 256, 16384], P('area', None, 'tile'), may hold values from -0.8984375 to 0.8984375
- stim_drive: bfloat16 [16, 256, 16384], P('area', None, 'tile'), may hold values from -6 to 6
- leak_rates: float32 [16, 16384], P('area', 'tile'), may hold values from 0.2 to 0.9
- block_weights: bfloat16 [16, 128, 20, 128, 128], P('area', 'tile'), may hold values from -0.21875 to 0.21875
- near_index: int32 [16, 128, 12], P('area', 'tile'), may hold values from 0 to 9, as said below
- far_index: int32 [16, 128, 8], P('area', 'tile'), may hold values from 0 to 15, as said below
Outputs:
- final_rates: bfloat16 [16, 256, 16384], P('area', None, 'tile')
The draws below stay inside these ranges and needn't reach their ends.
Inputs may be any that keep to these rules, and one draw needn't show every extreme that they name: `near_index`: an entry names one of the tile's own blocks (1 to 8) or the adjacent edge block of the neighbouring tile (0 the lower, 9 the upper). Slot 0 of every tile's first row block is 0 and slot 1 of every tile's last row block is 9. `far_index`: an entry q names the projecting block (the first block) of the same tile in section q, a section of another area; the areas are the consecutive groups of 3, 2, 2 and 1 eighths of the sections, in that order.
All inputs are finite; a program needn't handle non-finite values.
Results may differ from the reference program's by a relative error of at most 0.005.
Values may be sent and summed in bfloat16 or wider, within the bound.
No kernel may reach another device: no remote copies, remote signals or barrier semaphores. Data moves between devices by JAX's collectives and lax.ppermute only.
A program may use at most 64 MiB of HBM per device.

```python
import jax
import jax.numpy as jnp
from jax import lax

BLK = 128
RB = 8
K_REC = 12
K_INT = 8
EXPORT = 1
STEPS = 3
BATCH = 256
NEURONS = 16384
N_AREA = 16
N_TILE = 16


def draw_near_index(key, part):
    row_count = N_TILE * RB
    slot_values = jax.random.randint(key, (N_AREA, row_count, K_REC), 0, RB + 2)
    within = jnp.arange(row_count) % RB
    slot_number = jnp.arange(K_REC)
    first_block = (within == 0)[None, :, None] & (slot_number == 0)[None, None, :]
    last_block = (within == RB - 1)[None, :, None] & (slot_number == 1)[None, None, :]
    slot_values = jnp.where(first_block, 0, slot_values)
    slot_values = jnp.where(last_block, RB + 1, slot_values)
    return slot_values.astype(jnp.int32)


def draw_far_index(key, part):
    unit_size = N_AREA // 8
    device_ids = jnp.arange(N_AREA)
    group_start = jnp.where(device_ids >= 7 * unit_size, 7 * unit_size, jnp.where(device_ids >= 5 * unit_size, 5 * unit_size, jnp.where(device_ids >= 3 * unit_size, 3 * unit_size, 0)))
    group_end = jnp.where(device_ids >= 7 * unit_size, 8 * unit_size, jnp.where(device_ids >= 5 * unit_size, 7 * unit_size, jnp.where(device_ids >= 3 * unit_size, 5 * unit_size, 3 * unit_size)))
    own_count = group_end - group_start
    key_device, key_export = jax.random.split(key)
    shape_all = (N_AREA, N_TILE * RB, K_INT)
    upper_bound = jnp.broadcast_to((N_AREA - own_count)[:, None, None], shape_all)
    drawn_rank = jax.random.randint(key_device, shape_all, 0, upper_bound)
    source_device = jnp.where(drawn_rank < group_start[:, None, None], drawn_rank, drawn_rank + own_count[:, None, None])
    export_pick = jax.random.randint(key_export, shape_all, 0, EXPORT)
    return (source_device * EXPORT + export_pick).astype(jnp.int32)


def level_of(stream_key, shape, pieces, smallest, high):
    def one(position, shards_of):
        heights = jax.random.uniform(jax.random.fold_in(jax.random.fold_in(stream_key, 6), position), (shards_of,), jnp.float32, smallest / len(pieces), high / len(pieces))
        return jnp.repeat(jnp.exp(heights), shape[position] // shards_of).reshape((-1,) + (1,) * (len(shape) - position - 1))

    loudness = one(*pieces[0])
    for cut in pieces[1:]:
        loudness = loudness * one(*cut)
    return loudness


def gaussian(stream_key, shape, spread, most, shards=(), kind=jnp.bfloat16):
    result = spread * jax.random.normal(stream_key, shape, jnp.float32)
    if shards:
        result = result * level_of(stream_key, shape, shards, -0.22, 0.18)
    return jnp.clip(result, -most, most).astype(kind)


def setup_inputs(seed: int = 0) -> dict:
    key_list = jax.random.split(jax.random.key(seed), 7)
    start_rates = jnp.clip(jax.random.uniform(key_list[0], (N_AREA, BATCH, NEURONS), jnp.float32, -0.8984375, 0.8984375) * level_of(key_list[0], (N_AREA, BATCH, NEURONS), ((0, 16), (2, 16)), -0.4, 0.0), -0.8984375, 0.8984375).astype(jnp.bfloat16)
    stim_drive = gaussian(key_list[1], (N_AREA, BATCH, NEURONS), 1.0, 6.0, ((0, 16), (2, 16)))
    leak_rates = jnp.clip(0.2 + 0.7 * jax.random.uniform(key_list[2], (N_AREA, NEURONS), jnp.float32) ** level_of(key_list[2], (N_AREA, NEURONS), ((0, 16), (1, 16)), -0.2, 0.2), 0.2, 0.9)
    block_weights = gaussian(key_list[3], (N_AREA, N_TILE * RB, K_REC + K_INT, BLK, BLK), ((K_REC + K_INT) * BLK // 3) ** -0.5, 0.21875, ((0, 16), (1, 16)))
    near_index = draw_near_index(jax.random.fold_in(key_list[6], 71), 0)
    far_index = draw_far_index(jax.random.fold_in(key_list[6], 71), 0)
    return dict(start_rates=start_rates, stim_drive=stim_drive, leak_rates=leak_rates, block_weights=block_weights, near_index=near_index, far_index=far_index)


def reference(start_rates, stim_drive, leak_rates, block_weights, near_index, far_index):
    block_count = N_TILE * RB
    tile_number = jnp.arange(block_count, dtype=jnp.int32) // RB
    near_column = (tile_number * RB)[None, :, None] + near_index
    far_column = (tile_number * (N_AREA * EXPORT))[None, :, None] + far_index
    rates_now = start_rates
    for step_index in range(STEPS):
        grouped = rates_now.reshape(N_AREA, BATCH, N_TILE, RB, BLK)[:, :, :, :EXPORT, :]
        export_pool = jnp.transpose(grouped, (1, 2, 0, 3, 4)).reshape(BATCH, N_TILE * N_AREA * EXPORT, BLK)

        def one_area(area_number):
            area_rates = rates_now[area_number].reshape(BATCH, block_count, BLK)
            edge_zero = jnp.zeros((BATCH, 1, BLK), jnp.bfloat16)
            padded = jnp.concatenate((edge_zero, area_rates, edge_zero), axis=1)
            near_selected = jnp.take(padded, near_column[area_number], axis=1)
            far_selected = jnp.take(export_pool, far_column[area_number], axis=1)
            selected = jnp.concatenate((near_selected, far_selected), axis=2).astype(jnp.float32)
            current = jnp.einsum("brki,rkio->bro", selected, block_weights[area_number].astype(jnp.float32))
            current = current.reshape(BATCH, -1) + stim_drive[area_number].astype(jnp.float32)
            leak_now = leak_rates[area_number]
            updated = (1.0 - leak_now) * rates_now[area_number].astype(jnp.float32) + leak_now * jnp.tanh(current)
            return updated.astype(jnp.bfloat16)

        rates_now = lax.map(one_area, jnp.arange(N_AREA, dtype=jnp.int32))
    return rates_now
```

```python
import functools

import jax
import jax.numpy as jnp
from jax import lax
from jax.experimental import pallas as pl
from jax.experimental.pallas import tpu as pltpu
from jax.sharding import PartitionSpec as P

STEPS = 3
AREAS = 16
RING = 8
TILES = 16
VMEM = pl.BlockSpec(memory_space=pltpu.VMEM)
SMEM = pl.BlockSpec(memory_space=pltpu.SMEM)
PARAMS = pltpu.CompilerParams(vmem_limit_bytes=40 * 1024 * 1024)


def first_way(z, t):
    return 1 if (z + t) % 2 == 0 else -1


def pairs_of(where):
    pairs = []
    for x in range(AREAS // RING):
        for z in range(RING):
            for t in range(TILES):
                to_x, to_z = where(x, z, t)
                pairs.append(((x * RING + z) * TILES + t, (to_x * RING + to_z) * TILES + t))
    return pairs


NEAR_FIRST = pairs_of(lambda x, z, t: (x, (z + first_way(z, t)) % RING))
NEAR_SECOND = pairs_of(lambda x, z, t: (x, (z - first_way(z, t)) % RING))
ACROSS = pairs_of(lambda x, z, t: (1 - x, z))
TILE_INSIDE = [(t, t ^ 1) for t in range(TILES)]
TILE_OUTSIDE = [(t, t + 1) for t in range(1, TILES - 1, 2)] + [
    (t, t - 1) for t in range(2, TILES, 2)
]


def send(array, pairs):
    return lax.ppermute(array, ("area", "tile"), pairs)


def gather_exports(own):
    r1 = send(own, NEAR_FIRST)
    c2 = jnp.stack([own, r1])
    r2 = send(c2, NEAR_SECOND)
    qa = send(c2, ACROSS)
    r3 = send(r2, NEAR_FIRST)
    qb = send(r2, ACROSS)
    r4 = send(r3, NEAR_SECOND)
    qc = send(r3, ACROSS)
    qd = send(r4, ACROSS)
    return (c2, r2, r3, r4, qa, qb, qc, qd)


def near_kernel(near_count, index, rates, inner, outer, weights, drive, out, pool):
    blk = inner.shape[-1]
    rows = weights.shape[0]
    for j in range(rows):
        pool[j] = rates[:, j * blk : (j + 1) * blk]
    pool[rows] = inner[...]
    pool[rows + 1] = outer[...]
    for c in range(rows):
        left = jnp.concatenate([pool[index[c, k]] for k in range(near_count)], axis=1)
        right = weights[c, :near_count].reshape(near_count * blk, blk)
        lanes = slice(c * blk, (c + 1) * blk)
        out[:, lanes] = jnp.dot(
            left, right, preferred_element_type=jnp.float32
        ) + drive[:, lanes].astype(jnp.float32)


def far_rows(near_count, first, last, index, pool, weights, partial, rates, leak, write):
    blk = weights.shape[-1]
    total = weights.shape[1]
    for c in range(first, last):
        left = jnp.concatenate(
            [pool[index[c, k]] for k in range(total - near_count)], axis=1
        )
        right = weights[c, near_count:].reshape((total - near_count) * blk, blk)
        lanes = slice(c * blk, (c + 1) * blk)
        current = partial[:, lanes] + jnp.dot(left, right, preferred_element_type=jnp.float32)
        pace = leak[:, lanes]
        updated = (1.0 - pace) * rates[:, lanes].astype(jnp.float32) + pace * jnp.tanh(current)
        write(c, updated.astype(jnp.bfloat16))


def fill(pool, parts):
    for number, part in enumerate(parts):
        pool[2 * number] = part[0]
        pool[2 * number + 1] = part[1]


def export_kernel(near_count, index, *refs):
    parts, (weights, partial, rates, leak, out, pool) = refs[:8], refs[8:]
    fill(pool, parts)

    def write(c, value):
        out[...] = value

    far_rows(near_count, 0, 1, index, pool, weights, partial, rates, leak, write)


def rest_kernel(near_count, index, *refs):
    parts, (weights, partial, rates, leak, export, out, pool) = refs[:8], refs[8:]
    blk = weights.shape[-1]
    fill(pool, parts)
    out[:, :blk] = export[...]

    def write(c, value):
        out[:, c * blk : (c + 1) * blk] = value

    far_rows(near_count, 1, weights.shape[0], index, pool, weights, partial, rates, leak, write)


def whole_kernel(near_count, index, *refs):
    parts, (weights, partial, rates, leak, out, pool) = refs[:8], refs[8:]
    blk = weights.shape[-1]
    fill(pool, parts)

    def write(c, value):
        out[:, c * blk : (c + 1) * blk] = value

    far_rows(near_count, 0, weights.shape[0], index, pool, weights, partial, rates, leak, write)


def body(start_rates, stim_drive, leak_rates, block_weights, near_index, far_index):
    rates = start_rates[0]
    drive = stim_drive[0]
    leak = leak_rates
    weights = block_weights[0]
    near_index = near_index[0]
    far_index = far_index[0]
    batch, width = rates.shape
    rows, slots, blk, _ = weights.shape
    near_count = near_index.shape[1]
    far_count = far_index.shape[1]

    area, tile = lax.axis_index("area"), lax.axis_index("tile")
    my_x, my_z = area // RING, area % RING
    core = tile % 2
    near_at = jnp.where(
        near_index == 0, rows + 1 - core, jnp.where(near_index == rows + 1, rows + core, near_index - 1)
    )
    way = jnp.where((my_z + tile) % 2 == 0, 1, -1)
    off = ((far_index % RING - my_z) * way) % RING
    arrival = jnp.zeros_like(off)
    for place, distance in enumerate((0, 1, 7, 6, 2, 3, 5, 4)):
        arrival = jnp.where(off == distance, place, arrival)
    far_at = arrival + RING * (far_index // RING != my_x).astype(jnp.int32)

    def cost(row_blocks, count):
        return pl.CostEstimate(
            flops=2 * batch * blk * blk * row_blocks * count,
            bytes_accessed=2 * blk * blk * row_blocks * count + batch * width * 4,
            transcendentals=0,
        )

    near_call = pl.pallas_call(
        functools.partial(near_kernel, near_count),
        out_shape=jax.ShapeDtypeStruct((batch, width), jnp.float32),
        in_specs=[SMEM] + [VMEM] * 5,
        out_specs=VMEM,
        scratch_shapes=[pltpu.VMEM((rows + 2, batch, blk), jnp.bfloat16)],
        compiler_params=PARAMS,
        cost_estimate=cost(rows, near_count),
        name="near",
    )

    def far_call(kernel, out_width, operands, row_blocks, name):
        return pl.pallas_call(
            functools.partial(kernel, near_count),
            out_shape=jax.ShapeDtypeStruct((batch, out_width), jnp.bfloat16),
            in_specs=[SMEM] + [VMEM] * operands,
            out_specs=VMEM,
            scratch_shapes=[pltpu.VMEM((AREAS, batch, blk), jnp.bfloat16)],
            compiler_params=PARAMS,
            cost_estimate=cost(row_blocks, far_count),
            name=name,
        )

    export_call = far_call(export_kernel, blk, 12, 1, "export")
    rest_call = far_call(rest_kernel, width, 13, rows - 1, "rest")
    whole_call = far_call(whole_kernel, width, 12, rows, "whole")

    export = rates[:, :blk]
    for step in range(STEPS):
        first, last = rates[:, :blk], rates[:, width - blk :]
        inner = lax.ppermute(jnp.where(core == 0, last, first), "tile", TILE_INSIDE)
        outer = lax.ppermute(jnp.where(core == 0, first, last), "tile", TILE_OUTSIDE)
        parts = gather_exports(export)
        partial = near_call(near_at, rates, inner, outer, weights, drive)
        if step < STEPS - 1:
            export = export_call(far_at, *parts, weights, partial, rates, leak)
            rates = rest_call(far_at, *parts, weights, partial, rates, leak, export)
        else:
            rates = whole_call(far_at, *parts, weights, partial, rates, leak)
    return rates[None]


def solution(mesh):
    in_specs = (
        P("area", None, "tile"),
        P("area", None, "tile"),
        P("area", "tile"),
        P("area", "tile", None, None, None),
        P("area", "tile", None),
        P("area", "tile", None),
    )
    out_specs = P("area", None, "tile")
    return jax.shard_map(body, mesh=mesh, in_specs=in_specs, out_specs=out_specs, check_vma=False)
```

```python
import functools

import jax
import jax.numpy as jnp
from jax import lax
from jax.experimental import pallas as pl
from jax.experimental.pallas import tpu as pltpu
from jax.sharding import PartitionSpec as P

STEPS = 3
AREAS = 16
RING = 8
TILES = 16
PARTS = 8
VMEM = pl.BlockSpec(memory_space=pltpu.VMEM)
SMEM = pl.BlockSpec(memory_space=pltpu.SMEM)
PARAMS = pltpu.CompilerParams(vmem_limit_bytes=40 * 1024 * 1024)


def first_way(z, t):
    return 1 if (z + t) % 2 == 0 else -1


def pairs_of(where):
    pairs = []
    for x in range(AREAS // RING):
        for z in range(RING):
            for t in range(TILES):
                to_x, to_z = where(x, z, t)
                pairs.append(((x * RING + z) * TILES + t, (to_x * RING + to_z) * TILES + t))
    return pairs


NEAR_FIRST = pairs_of(lambda x, z, t: (x, (z + first_way(z, t)) % RING))
NEAR_SECOND = pairs_of(lambda x, z, t: (x, (z - first_way(z, t)) % RING))
ACROSS = pairs_of(lambda x, z, t: (1 - x, z))
ACROSS_SECOND = pairs_of(lambda x, z, t: (1 - x, (z - first_way(z, t)) % RING))
TILE_INSIDE = [(t, t ^ 1) for t in range(TILES)]
TILE_OUTSIDE = [(t, t + 1) for t in range(1, TILES - 1, 2)] + [
    (t, t - 1) for t in range(2, TILES, 2)
]


def send(array, pairs):
    return lax.ppermute(array, ("area", "tile"), pairs)


def after(array, *others):
    return lax.optimization_barrier((array, *others))[0]


def near_kernel(near_count, place, index, rates, inner, outer, weights, drive, out, pool):
    blk = inner.shape[-1]
    rows = weights.shape[0]
    odd = place[2]
    for j in range(rows):
        pool[j + 1] = rates[:, j * blk : (j + 1) * blk]
    pool[(1 - odd) * (rows + 1)] = inner[...]
    pool[odd * (rows + 1)] = outer[...]
    for c in range(rows):
        left = jnp.concatenate([pool[index[c, k]] for k in range(near_count)], axis=1)
        right = weights[c, :near_count].reshape(near_count * blk, blk)
        lanes = slice(c * blk, (c + 1) * blk)
        out[:, lanes] = jnp.dot(
            left, right, preferred_element_type=jnp.float32
        ) + drive[:, lanes].astype(jnp.float32)


def bring_kernel(place, *refs):
    out = refs[-1]
    for i in range(place.shape[0]):
        out[i] = place[i]


def far_row(near_count, c, index, pool, weights, partial, rates, leak):
    blk = weights.shape[-1]
    total = weights.shape[1]
    left = jnp.concatenate([pool[index[c, k]] for k in range(total - near_count)], axis=1)
    right = weights[c, near_count:].reshape((total - near_count) * blk, blk)
    lanes = slice(c * blk, (c + 1) * blk)
    current = partial[:, lanes] + jnp.dot(left, right, preferred_element_type=jnp.float32)
    pace = leak[:, lanes]
    updated = (1.0 - pace) * rates[:, lanes].astype(jnp.float32) + pace * jnp.tanh(current)
    return updated.astype(jnp.bfloat16)


def fill(pool, place, parts):
    mine, z, odd = place[0], place[1], place[2]
    way = 1 - 2 * ((z + odd) % 2)
    for number, part in enumerate(parts):
        plane = mine if number < 4 else RING - mine
        for half, distance in enumerate(((0, 1), (-1, -2), (2, 3), (-3, -4))[number % 4]):
            pool[plane + (z + way * distance + RING) % RING] = part[half]


def export_kernel(near_count, place, index, *refs):
    parts, (weights, partial, rates, leak, first, inside, outside, pool) = (
        refs[:PARTS],
        refs[PARTS:],
    )
    fill(pool, place, parts)
    odd = place[2]
    lead, trail = (
        far_row(near_count, c, index, pool, weights, partial, rates, leak)
        for c in (0, weights.shape[0] - 1)
    )
    first[...] = lead
    inside[...] = jnp.where(odd == 0, trail, lead)
    outside[...] = jnp.where(odd == 0, lead, trail)


def rest_kernel(near_count, place, index, *refs):
    parts, (weights, partial, rates, leak, first, inside, outside, out, pool) = (
        refs[:PARTS],
        refs[PARTS:],
    )
    blk = weights.shape[-1]
    rows = weights.shape[0]
    fill(pool, place, parts)
    odd = place[2]
    out[:, :blk] = first[...]
    out[:, (rows - 1) * blk :] = jnp.where(odd == 0, inside[...], outside[...])
    for c in range(1, rows - 1):
        out[:, c * blk : (c + 1) * blk] = far_row(
            near_count, c, index, pool, weights, partial, rates, leak
        )


def whole_kernel(near_count, place, index, *refs):
    parts, (weights, partial, rates, leak, out, pool) = refs[:PARTS], refs[PARTS:]
    blk = weights.shape[-1]
    fill(pool, place, parts)
    for c in range(weights.shape[0]):
        out[:, c * blk : (c + 1) * blk] = far_row(
            near_count, c, index, pool, weights, partial, rates, leak
        )


def body(start_rates, stim_drive, leak_rates, block_weights, near_index, far_index):
    rates = start_rates[0]
    drive = stim_drive[0]
    leak = leak_rates
    weights = block_weights[0]
    near_index = near_index[0]
    far_index = far_index[0]
    batch, width = rates.shape
    rows, slots, blk, _ = weights.shape
    near_count = near_index.shape[1]
    far_count = far_index.shape[1]

    area, tile = lax.axis_index("area"), lax.axis_index("tile")
    core = tile % 2
    place = jnp.stack([area // RING * RING, area % RING, core])

    def cost(row_blocks, count):
        return pl.CostEstimate(
            flops=2 * batch * blk * blk * row_blocks * count,
            bytes_accessed=2 * blk * blk * row_blocks * count + batch * width * 4,
            transcendentals=0,
        )

    near_call = pl.pallas_call(
        functools.partial(near_kernel, near_count),
        out_shape=jax.ShapeDtypeStruct((batch, width), jnp.float32),
        in_specs=[SMEM, SMEM] + [VMEM] * 5,
        out_specs=VMEM,
        scratch_shapes=[pltpu.VMEM((rows + 2, batch, blk), jnp.bfloat16)],
        compiler_params=PARAMS,
        cost_estimate=cost(rows, near_count),
        name="near",
    )

    def bring(place, *arrays):
        specs = [SMEM if array.dtype == jnp.int32 else VMEM for array in (place, *arrays)]
        return pl.pallas_call(
            bring_kernel,
            out_shape=jax.ShapeDtypeStruct(place.shape, place.dtype),
            in_specs=specs,
            out_specs=SMEM,
            compiler_params=PARAMS,
            name="bring",
        )(place, *arrays)

    def far_call(kernel, outs, operands, row_blocks, name):
        shapes = [jax.ShapeDtypeStruct((batch, lanes), jnp.bfloat16) for lanes in outs]
        return pl.pallas_call(
            functools.partial(kernel, near_count),
            out_shape=shapes if len(shapes) > 1 else shapes[0],
            in_specs=[SMEM, SMEM] + [VMEM] * (PARTS + operands),
            out_specs=[VMEM] * len(shapes) if len(shapes) > 1 else VMEM,
            scratch_shapes=[pltpu.VMEM((AREAS, batch, blk), jnp.bfloat16)],
            compiler_params=PARAMS,
            cost_estimate=cost(row_blocks, far_count),
            name=name,
        )

    export_call = far_call(export_kernel, [blk] * 3, 4, 2, "export")
    rest_call = far_call(rest_kernel, [width], 7, rows - 2, "rest")
    whole_call = far_call(whole_kernel, [width], 4, rows, "whole")

    lead, trail = rates[:, :blk], rates[:, width - blk :]
    export = lead
    inside, outside = jnp.where(core == 0, trail, lead), jnp.where(core == 0, lead, trail)
    for step in range(STEPS):
        r1 = send(export, NEAR_FIRST)
        inner = lax.ppermute(inside, "tile", TILE_INSIDE)
        outer = lax.ppermute(outside, "tile", TILE_OUTSIDE)
        if step:
            rates = rest_call(
                place, far_index, *parts, weights, partial, rates, leak, export, inside, outside
            )
            r1 = after(r1, rates, inner)
        else:
            place = bring(place, weights, near_index)
            r1 = after(r1, place, inner)
        c2 = jnp.stack([export, r1])
        r2 = send(c2, NEAR_SECOND)
        qa = send(c2, ACROSS)
        if not step:
            place = bring(place, rates, drive)
        r2 = after(r2, place)
        r3 = send(r2, NEAR_FIRST)
        qb = send(r2, ACROSS)
        partial = near_call(place, near_index, rates, inner, outer, weights, drive)
        r3 = after(r3, qa, qb)
        qd = send(r3, ACROSS_SECOND)
        r4 = send(r3, NEAR_SECOND)
        qc = send(r3, ACROSS)
        parts = (c2, r2, r3, r4, qa, qb, qc, qd)
        if step < STEPS - 1:
            export, inside, outside = export_call(
                place, far_index, *parts, weights, partial, rates, leak
            )
        else:
            rates = whole_call(place, far_index, *parts, weights, partial, rates, leak)
    return rates[None]


def solution(mesh):
    in_specs = (
        P("area", None, "tile"),
        P("area", None, "tile"),
        P("area", "tile"),
        P("area", "tile", None, None, None),
        P("area", "tile", None),
        P("area", "tile", None),
    )
    out_specs = P("area", None, "tile")
    return jax.shard_map(body, mesh=mesh, in_specs=in_specs, out_specs=out_specs, check_vma=False)
```

```python
import functools

import jax
import jax.numpy as jnp
from jax import lax
from jax.experimental import pallas as pl
from jax.experimental.pallas import tpu as pltpu
from jax.sharding import PartitionSpec as P

STEPS = 3
AREAS = 16
RING = 8
TILES = 16
PARTS = 8
VMEM = pl.BlockSpec(memory_space=pltpu.VMEM)
SMEM = pl.BlockSpec(memory_space=pltpu.SMEM)
PARAMS = pltpu.CompilerParams(vmem_limit_bytes=40 * 1024 * 1024)


def phase(t):
    return (t + 1) // 2 % 2


def first_way(z, t):
    return 1 if (z + phase(t)) % 2 == 0 else -1


def pairs_of(where):
    pairs = []
    for x in range(AREAS // RING):
        for z in range(RING):
            for t in range(TILES):
                to_x, to_z = where(x, z, t)
                pairs.append(((x * RING + z) * TILES + t, (to_x * RING + to_z) * TILES + t))
    return pairs


NEAR_FIRST = pairs_of(lambda x, z, t: (x, (z + first_way(z, t)) % RING))
NEAR_SECOND = pairs_of(lambda x, z, t: (x, (z - first_way(z, t)) % RING))
ACROSS = pairs_of(lambda x, z, t: (1 - x, z))
ACROSS_SECOND = pairs_of(lambda x, z, t: (1 - x, (z - first_way(z, t)) % RING))
TILE_INSIDE = [(t, t ^ 1) for t in range(TILES)]
TILE_OUTSIDE = [(t, t + 1) for t in range(1, TILES - 1, 2)] + [
    (t, t - 1) for t in range(2, TILES, 2)
]


def send(array, pairs):
    return lax.ppermute(array, ("area", "tile"), pairs)


def after(array, *others):
    return lax.optimization_barrier((array, *others))[0]


def near_kernel(near_count, place, index, rates, inner, outer, weights, drive, token, out, pool):
    blk = inner.shape[-1]
    rows = weights.shape[0]
    odd = place[2]
    for j in range(rows):
        pool[j + 1] = rates[:, j * blk : (j + 1) * blk]
    pool[(1 - odd) * (rows + 1)] = inner[...]
    pool[odd * (rows + 1)] = outer[...]
    for c in range(rows):
        left = jnp.concatenate([pool[index[c, k]] for k in range(near_count)], axis=1)
        right = weights[c, :near_count].reshape(near_count * blk, blk)
        lanes = slice(c * blk, (c + 1) * blk)
        out[:, lanes] = jnp.dot(
            left, right, preferred_element_type=jnp.float32
        ) + drive[:, lanes].astype(jnp.float32)


def bring_kernel(*refs):
    refs[-1][...] = jnp.zeros_like(refs[-1])


def far_row(near_count, c, index, pool, weights, partial, rates, leak):
    blk = weights.shape[-1]
    total = weights.shape[1]
    left = jnp.concatenate([pool[index[c, k]] for k in range(total - near_count)], axis=1)
    right = weights[c, near_count:].reshape((total - near_count) * blk, blk)
    lanes = slice(c * blk, (c + 1) * blk)
    current = partial[:, lanes] + jnp.dot(left, right, preferred_element_type=jnp.float32)
    pace = leak[:, lanes]
    updated = (1.0 - pace) * rates[:, lanes].astype(jnp.float32) + pace * jnp.tanh(current)
    return updated.astype(jnp.bfloat16)


def fill(pool, place, parts):
    mine, z = place[0], place[1]
    way = 1 - 2 * ((z + place[3]) % 2)
    for number, part in enumerate(parts):
        plane = mine if number < 4 else RING - mine
        for half, distance in enumerate(((0, 1), (-1, -2), (2, 3), (-3, -4))[number % 4]):
            pool[plane + (z + way * distance + RING) % RING] = part[half]


def export_kernel(near_count, place, index, *refs):
    parts, (weights, partial, rates, leak, first, inside, outside, pool) = (
        refs[:PARTS],
        refs[PARTS:],
    )
    fill(pool, place, parts)
    odd = place[2]
    lead, trail = (
        far_row(near_count, c, index, pool, weights, partial, rates, leak)
        for c in (0, weights.shape[0] - 1)
    )
    first[...] = lead
    inside[...] = jnp.where(odd == 0, trail, lead)
    outside[...] = jnp.where(odd == 0, lead, trail)


def rest_kernel(near_count, place, index, *refs):
    parts, (weights, partial, rates, leak, first, inside, outside, out, pool) = (
        refs[:PARTS],
        refs[PARTS:],
    )
    blk = weights.shape[-1]
    rows = weights.shape[0]
    fill(pool, place, parts)
    odd = place[2]
    out[:, :blk] = first[...]
    out[:, (rows - 1) * blk :] = jnp.where(odd == 0, inside[...], outside[...])
    for c in range(1, rows - 1):
        out[:, c * blk : (c + 1) * blk] = far_row(
            near_count, c, index, pool, weights, partial, rates, leak
        )


def whole_kernel(near_count, place, index, *refs):
    parts, (weights, partial, rates, leak, out, pool) = refs[:PARTS], refs[PARTS:]
    blk = weights.shape[-1]
    fill(pool, place, parts)
    for c in range(weights.shape[0]):
        out[:, c * blk : (c + 1) * blk] = far_row(
            near_count, c, index, pool, weights, partial, rates, leak
        )


def body(start_rates, stim_drive, leak_rates, block_weights, near_index, far_index):
    rates = start_rates[0]
    drive = stim_drive[0]
    leak = leak_rates
    weights = block_weights[0]
    near_index = near_index[0]
    far_index = far_index[0]
    batch, width = rates.shape
    rows, slots, blk, _ = weights.shape
    near_count = near_index.shape[1]
    far_count = far_index.shape[1]

    area, tile = lax.axis_index("area"), lax.axis_index("tile")
    core = tile % 2
    place = jnp.stack([area // RING * RING, area % RING, core, phase(tile)])

    def cost(row_blocks, count):
        return pl.CostEstimate(
            flops=2 * batch * blk * blk * row_blocks * count,
            bytes_accessed=2 * blk * blk * row_blocks * count + batch * width * 4,
            transcendentals=0,
        )

    near_call = pl.pallas_call(
        functools.partial(near_kernel, near_count),
        out_shape=jax.ShapeDtypeStruct((batch, width), jnp.float32),
        in_specs=[SMEM, SMEM] + [VMEM] * 6,
        out_specs=VMEM,
        scratch_shapes=[pltpu.VMEM((rows + 2, batch, blk), jnp.bfloat16)],
        compiler_params=PARAMS,
        cost_estimate=cost(rows, near_count),
        name="near",
    )

    def bring(*arrays):
        return pl.pallas_call(
            bring_kernel,
            out_shape=jax.ShapeDtypeStruct((8, blk), jnp.float32),
            in_specs=[SMEM if array.dtype == jnp.int32 else VMEM for array in arrays],
            out_specs=VMEM,
            compiler_params=PARAMS,
            cost_estimate=pl.CostEstimate(flops=1, bytes_accessed=12 * batch * width * rows, transcendentals=0),
            name="bring",
        )(*arrays)

    def far_call(kernel, outs, operands, row_blocks, name):
        shapes = [jax.ShapeDtypeStruct((batch, lanes), jnp.bfloat16) for lanes in outs]
        return pl.pallas_call(
            functools.partial(kernel, near_count),
            out_shape=shapes if len(shapes) > 1 else shapes[0],
            in_specs=[SMEM, SMEM] + [VMEM] * (PARTS + operands),
            out_specs=[VMEM] * len(shapes) if len(shapes) > 1 else VMEM,
            scratch_shapes=[pltpu.VMEM((AREAS, batch, blk), jnp.bfloat16)],
            compiler_params=PARAMS,
            cost_estimate=cost(row_blocks, far_count),
            name=name,
        )

    export_call = far_call(export_kernel, [blk] * 3, 4, 2, "export")
    rest_call = far_call(rest_kernel, [width], 7, rows - 2, "rest")
    whole_call = far_call(whole_kernel, [width], 4, rows, "whole")

    lead, trail = rates[:, :blk], rates[:, width - blk :]
    export = lead
    inside, outside = jnp.where(core == 0, trail, lead), jnp.where(core == 0, lead, trail)
    for step in range(STEPS):
        r1 = send(export, NEAR_FIRST)
        inner = lax.ppermute(inside, "tile", TILE_INSIDE)
        outer = lax.ppermute(outside, "tile", TILE_OUTSIDE)
        if step:
            rates = rest_call(
                place, far_index, *parts, weights, partial, rates, leak, export, inside, outside
            )
            r1 = after(r1, rates, inner)
        else:
            token = bring(weights)
            r1 = after(r1, token, inner)
        c2 = jnp.stack([export, r1])
        r2 = send(c2, NEAR_SECOND)
        qa = send(c2, ACROSS)
        if not step:
            token = bring(token, rates, drive)
        r2 = after(r2, token)
        r3 = send(r2, NEAR_FIRST)
        qb = send(r2, ACROSS)
        partial = near_call(place, near_index, rates, inner, outer, weights, drive, token)
        r3 = after(r3, qa, qb)
        qd = send(r3, ACROSS_SECOND)
        r4 = send(r3, NEAR_SECOND)
        qc = send(r3, ACROSS)
        parts = (c2, r2, r3, r4, qa, qb, qc, qd)
        if step < STEPS - 1:
            export, inside, outside = export_call(
                place, far_index, *parts, weights, partial, rates, leak
            )
        else:
            rates = whole_call(place, far_index, *parts, weights, partial, rates, leak)
    return rates[None]


def solution(mesh):
    in_specs = (
        P("area", None, "tile"),
        P("area", None, "tile"),
        P("area", "tile"),
        P("area", "tile", None, None, None),
        P("area", "tile", None),
        P("area", "tile", None),
    )
    out_specs = P("area", None, "tile")
    return jax.shard_map(body, mesh=mesh, in_specs=in_specs, out_specs=out_specs, check_vma=False)
```

```python
import functools

import jax
import jax.numpy as jnp
from jax import lax
from jax.experimental import pallas as pl
from jax.experimental.pallas import tpu as pltpu
from jax.sharding import PartitionSpec as P

STEPS = 3
AREAS = 16
RING = 8
TILES = 16
PARTS = 8
VMEM = pl.BlockSpec(memory_space=pltpu.VMEM)
SMEM = pl.BlockSpec(memory_space=pltpu.SMEM)
PARAMS = pltpu.CompilerParams(vmem_limit_bytes=40 * 1024 * 1024)


def phase(t):
    return (t + 1) // 2 % 2


def first_way(z, t):
    return 1 if (z + phase(t)) % 2 == 0 else -1


def pairs_of(where):
    pairs = []
    for x in range(AREAS // RING):
        for z in range(RING):
            for t in range(TILES):
                to_x, to_z = where(x, z, t)
                pairs.append(((x * RING + z) * TILES + t, (to_x * RING + to_z) * TILES + t))
    return pairs


NEAR_FIRST = pairs_of(lambda x, z, t: (x, (z + first_way(z, t)) % RING))
NEAR_SECOND = pairs_of(lambda x, z, t: (x, (z - first_way(z, t)) % RING))
ACROSS = pairs_of(lambda x, z, t: (1 - x, z))
ACROSS_SECOND = pairs_of(lambda x, z, t: (1 - x, (z - first_way(z, t)) % RING))
TILE_INSIDE = [(t, t ^ 1) for t in range(TILES)]
TILE_OUTSIDE = [(t, t + 1) for t in range(1, TILES - 1, 2)] + [
    (t, t - 1) for t in range(2, TILES, 2)
]


def send(array, pairs):
    return lax.ppermute(array, ("area", "tile"), pairs)


def after(array, *others):
    return lax.optimization_barrier((array, *others))[0]


def near_kernel(near_count, place, index, rates, inner, outer, weights, drive, token, out, pool):
    blk = inner.shape[-1]
    rows = weights.shape[0]
    odd = place[2]
    for j in range(rows):
        pool[j + 1] = rates[:, j * blk : (j + 1) * blk]
    pool[(1 - odd) * (rows + 1)] = inner[...]
    pool[odd * (rows + 1)] = outer[...]
    for c in range(rows):
        left = jnp.concatenate([pool[index[c, k]] for k in range(near_count)], axis=1)
        right = weights[c, :near_count].reshape(near_count * blk, blk)
        lanes = slice(c * blk, (c + 1) * blk)
        out[:, lanes] = jnp.dot(
            left, right, preferred_element_type=jnp.float32
        ) + drive[:, lanes].astype(jnp.float32)


def bring_kernel(*refs):
    refs[-1][...] = jnp.zeros_like(refs[-1])


def far_row(near_count, c, index, pool, weights, partial, rates, leak):
    blk = weights.shape[-1]
    total = weights.shape[1]
    left = jnp.concatenate([pool[index[c, k]] for k in range(total - near_count)], axis=1)
    right = weights[c, near_count:].reshape((total - near_count) * blk, blk)
    lanes = slice(c * blk, (c + 1) * blk)
    current = partial[:, lanes] + jnp.dot(left, right, preferred_element_type=jnp.float32)
    pace = leak[:, lanes]
    updated = (1.0 - pace) * rates[:, lanes].astype(jnp.float32) + pace * jnp.tanh(current)
    return updated.astype(jnp.bfloat16)


def fill(pool, place, parts):
    mine, z = place[0], place[1]
    way = 1 - 2 * ((z + place[3]) % 2)
    for number, part in enumerate(parts):
        plane = mine if number < 4 else RING - mine
        for half, distance in enumerate(((0, 1), (-1, -2), (2, 3), (-3, -4))[number % 4]):
            pool[plane + (z + way * distance + RING) % RING] = part[half]


def export_kernel(near_count, place, index, *refs):
    parts, (weights, partial, rates, leak, first, inside, outside, pool) = (
        refs[:PARTS],
        refs[PARTS:],
    )
    fill(pool, place, parts)
    odd = place[2]
    lead, trail = (
        far_row(near_count, c, index, pool, weights, partial, rates, leak)
        for c in (0, weights.shape[0] - 1)
    )
    first[...] = lead
    inside[...] = jnp.where(odd == 0, trail, lead)
    outside[...] = jnp.where(odd == 0, lead, trail)


def rest_kernel(near_count, place, index, *refs):
    parts, (weights, partial, rates, leak, first, inside, outside, out, pool) = (
        refs[:PARTS],
        refs[PARTS:],
    )
    blk = weights.shape[-1]
    rows = weights.shape[0]
    fill(pool, place, parts)
    odd = place[2]
    out[:, :blk] = first[...]
    out[:, (rows - 1) * blk :] = jnp.where(odd == 0, inside[...], outside[...])
    for c in range(1, rows - 1):
        out[:, c * blk : (c + 1) * blk] = far_row(
            near_count, c, index, pool, weights, partial, rates, leak
        )


def whole_kernel(near_count, place, index, *refs):
    parts, (weights, partial, rates, leak, out, pool, held, sems) = refs[:PARTS], refs[PARTS:]
    blk = weights.shape[-1]
    fill(pool, place, parts)
    copies = []
    for c in range(weights.shape[0]):
        held[c] = far_row(near_count, c, index, pool, weights, partial, rates, leak)
        copy = pltpu.make_async_copy(held.at[c], out.at[:, pl.ds(c * blk, blk)], sems.at[c])
        copy.start()
        copies.append(copy)
    for copy in copies:
        copy.wait()


def body(start_rates, stim_drive, leak_rates, block_weights, near_index, far_index):
    rates = start_rates[0]
    drive = stim_drive[0]
    leak = leak_rates
    weights = block_weights[0]
    near_index = near_index[0]
    far_index = far_index[0]
    batch, width = rates.shape
    rows, slots, blk, _ = weights.shape
    near_count = near_index.shape[1]
    far_count = far_index.shape[1]

    area, tile = lax.axis_index("area"), lax.axis_index("tile")
    core = tile % 2
    place = jnp.stack([area // RING * RING, area % RING, core, phase(tile)])

    def cost(row_blocks, count):
        return pl.CostEstimate(
            flops=2 * batch * blk * blk * row_blocks * count,
            bytes_accessed=2 * blk * blk * row_blocks * count + batch * width * 4,
            transcendentals=0,
        )

    near_call = pl.pallas_call(
        functools.partial(near_kernel, near_count),
        out_shape=jax.ShapeDtypeStruct((batch, width), jnp.float32),
        in_specs=[SMEM, SMEM] + [VMEM] * 6,
        out_specs=VMEM,
        scratch_shapes=[pltpu.VMEM((rows + 2, batch, blk), jnp.bfloat16)],
        compiler_params=PARAMS,
        cost_estimate=cost(rows, near_count),
        name="near",
    )

    def bring(*arrays):
        return pl.pallas_call(
            bring_kernel,
            out_shape=jax.ShapeDtypeStruct((8, blk), jnp.float32),
            in_specs=[SMEM if array.dtype == jnp.int32 else VMEM for array in arrays],
            out_specs=VMEM,
            compiler_params=PARAMS,
            cost_estimate=pl.CostEstimate(flops=1, bytes_accessed=12 * batch * width * rows, transcendentals=0),
            name="bring",
        )(*arrays)

    def far_call(kernel, outs, operands, row_blocks, name):
        shapes = [jax.ShapeDtypeStruct((batch, lanes), jnp.bfloat16) for lanes in outs]
        return pl.pallas_call(
            functools.partial(kernel, near_count),
            out_shape=shapes if len(shapes) > 1 else shapes[0],
            in_specs=[SMEM, SMEM] + [VMEM] * (PARTS + operands),
            out_specs=[VMEM] * len(shapes) if len(shapes) > 1 else VMEM,
            scratch_shapes=[pltpu.VMEM((AREAS, batch, blk), jnp.bfloat16)],
            compiler_params=PARAMS,
            cost_estimate=cost(row_blocks, far_count),
            name=name,
        )

    export_call = far_call(export_kernel, [blk] * 3, 4, 2, "export")
    rest_call = far_call(rest_kernel, [width], 7, rows - 2, "rest")
    whole_call = pl.pallas_call(
        functools.partial(whole_kernel, near_count),
        out_shape=jax.ShapeDtypeStruct((batch, width), jnp.bfloat16),
        in_specs=[SMEM, SMEM] + [VMEM] * (PARTS + 4),
        out_specs=pl.BlockSpec(memory_space=pl.ANY),
        scratch_shapes=[
            pltpu.VMEM((AREAS, batch, blk), jnp.bfloat16),
            pltpu.VMEM((rows, batch, blk), jnp.bfloat16),
            pltpu.SemaphoreType.DMA((rows,)),
        ],
        compiler_params=PARAMS,
        cost_estimate=cost(rows, far_count),
        name="whole",
    )

    lead, trail = rates[:, :blk], rates[:, width - blk :]
    export = lead
    inside, outside = jnp.where(core == 0, trail, lead), jnp.where(core == 0, lead, trail)
    for step in range(STEPS):
        r1 = send(export, NEAR_FIRST)
        inner = lax.ppermute(inside, "tile", TILE_INSIDE)
        outer = lax.ppermute(outside, "tile", TILE_OUTSIDE)
        if step:
            rates = rest_call(
                place, far_index, *parts, weights, partial, rates, leak, export, inside, outside
            )
            r1 = after(r1, rates, inner)
        else:
            token = bring(weights)
            r1 = after(r1, token, inner)
        c2 = jnp.stack([export, r1])
        r2 = send(c2, NEAR_SECOND)
        qa = send(c2, ACROSS)
        if not step:
            token = bring(token, rates, drive)
        r2 = after(r2, token)
        r3 = send(r2, NEAR_FIRST)
        qb = send(r2, ACROSS)
        partial = near_call(place, near_index, rates, inner, outer, weights, drive, token)
        r3 = after(r3, qa, qb)
        qd = send(r3, ACROSS_SECOND)
        r4 = send(r3, NEAR_SECOND)
        qc = send(r3, ACROSS)
        parts = (c2, r2, r3, r4, qa, qb, qc, qd)
        if step < STEPS - 1:
            export, inside, outside = export_call(
                place, far_index, *parts, weights, partial, rates, leak
            )
        else:
            rates = whole_call(place, far_index, *parts, weights, partial, rates, leak)
    return rates[None]


def solution(mesh):
    in_specs = (
        P("area", None, "tile"),
        P("area", None, "tile"),
        P("area", "tile"),
        P("area", "tile", None, None, None),
        P("area", "tile", None),
        P("area", "tile", None),
    )
    out_specs = P("area", None, "tile")
    return jax.shard_map(body, mesh=mesh, in_specs=in_specs, out_specs=out_specs, check_vma=False)
```
